32 devices in a mesh: row: 8 (over z, x), col: 4 (over y, core).
Axes of the slice: x: 2, y: 2, z: 4, core: 2. Of those that a mesh axis runs over, the one named last changes fastest.
Arguments:
- tokens: bfloat16 [320, 8192], P('row', 'col'), may hold values from -6 to 6
- out_grad: bfloat16 [320, 8192], P('row', 'col'), may hold values from -1.5 to 1.5
- gate_saved: bfloat16 [320, 26624], P(None, 'row'), may hold values from -6 to 6
- up_saved: bfloat16 [320, 26624], P(None, 'row'), may hold values from -6 to 6
- gate_weight: bfloat16 [8192, 26624], P('col', 'row'), may hold values from -0.0625 to 0.0625
- up_weight: bfloat16 [8192, 26624], P('col', 'row'), may hold values from -0.0625 to 0.0625
- down_weight: bfloat16 [26624, 8192], P('row', 'col'), may hold values from -0.0390625 to 0.0390625
Outputs:
- input_grad: bfloat16 [320, 8192], P('row', 'col')
- gate_grad: bfloat16 [8192, 26624], P('col', 'row')
- up_grad: bfloat16 [8192, 26624], P('col', 'row')
- down_grad: bfloat16 [26624, 8192], P('row', 'col')
The draws below stay inside these ranges and needn't reach their ends.
All inputs are finite; a program needn't handle non-finite values.
Results may differ from the reference program's by a relative error of at most 0.022.
Values may be sent and summed in bfloat16 or wider, within the bound.
No kernel may reach another device: no remote copies, remote signals or barrier semaphores. Data moves between devices by JAX's collectives and lax.ppermute only.
A program may use at most 192 MiB of HBM per device.

```python
import jax
import jax.numpy as jnp

D = 8192
FF = 26624
TOKENS = 320


def levels(rng, extent, split, low, top_value):
    gain, own = 1.0, jax.random.fold_in(rng, 6)
    for dim, parts in split:
        heights = jnp.exp(jax.random.uniform(jax.random.fold_in(own, dim), (parts,), jnp.float32, low / len(split), top_value / len(split)))
        gain = gain * jnp.repeat(heights, extent[dim] // parts).reshape([-1 if axis == dim else 1 for axis in range(len(extent))])
    return gain


def noise(own_key, extent, spread, limit, split=(), held_as=jnp.bfloat16):
    entries = jax.random.normal(own_key, extent, jnp.float32) * spread
    if len(split) > 0:
        entries = levels(own_key, extent, split, -0.22, 0.18) * entries
    return jnp.clip(entries, min=-limit, max=limit).astype(held_as)


def setup_inputs(seed: int = 0) -> dict:
    key_list = jax.random.split(jax.random.key(seed), 8)
    return {
        "tokens": noise(key_list[0], (TOKENS, D), 1.0, 6.0, ((0, 8), (1, 4))),
        "out_grad": noise(key_list[1], (TOKENS, D), (TOKENS ** -0.25), 1.5, ((0, 8), (1, 4))),
        "gate_saved": noise(key_list[2], (TOKENS, FF), 1.0, 6.0, ((1, 8),)),
        "up_saved": noise(key_list[3], (TOKENS, FF), 1.0, 6.0, ((1, 8),)),
        "gate_weight": noise(key_list[4], (D, FF), D ** -0.5, 0.0625, ((0, 4), (1, 8))),
        "up_weight": noise(key_list[5], (D, FF), D ** -0.5, 0.0625, ((0, 4), (1, 8))),
        "down_weight": noise(key_list[6], (FF, D), FF ** -0.5, 0.0390625, ((0, 8), (1, 4))),
    }


def reference(tokens, out_grad, gate_saved, up_saved, gate_weight, up_weight, down_weight):
    gate = gate_saved.astype(jnp.float32)
    up = up_saved.astype(jnp.float32)
    grad_hidden = jnp.dot(out_grad, down_weight.T, preferred_element_type=jnp.float32)
    sigma = jax.nn.sigmoid(gate)
    silu_gate = gate * sigma
    hidden = (silu_gate * up).astype(jnp.bfloat16)
    grad_up = (grad_hidden * silu_gate).astype(jnp.bfloat16)
    grad_gate = (grad_hidden * up * sigma * (1.0 + gate * (1.0 - sigma))).astype(jnp.bfloat16)
    input_grad = jnp.dot(grad_gate, gate_weight.T, preferred_element_type=jnp.float32)
    input_grad = input_grad + jnp.dot(grad_up, up_weight.T, preferred_element_type=jnp.float32)
    gate_grad = jnp.dot(tokens.T, grad_gate, preferred_element_type=jnp.float32)
    up_grad = jnp.dot(tokens.T, grad_up, preferred_element_type=jnp.float32)
    down_grad = jnp.dot(hidden.T, out_grad, preferred_element_type=jnp.float32)
    return (input_grad.astype(jnp.bfloat16), gate_grad.astype(jnp.bfloat16),
            up_grad.astype(jnp.bfloat16), down_grad.astype(jnp.bfloat16))
```

```python
import jax
import jax.numpy as jnp
from jax import lax
from jax.experimental import pallas as pl
from jax.experimental.pallas import tpu as pltpu
from jax.sharding import PartitionSpec as P

BF = jnp.bfloat16
F32 = jnp.float32
NT = (((1,), (1,)), ((), ()))
TN = (((0,), (0,)), ((), ()))
MIB = 1 << 20


def dot(a, b, dims):
    return lax.dot_general(a, b, dims, preferred_element_type=F32)


def tile(size, most, step):
    for part in range(min(most, size) // step * step, 0, -step):
        if size % part == 0:
            return part
    return size


def call(kernel, scalars, args, in_specs, out_specs, out_shape, grid, cost, vmem):
    return pl.pallas_call(
        kernel,
        out_shape=out_shape,
        grid_spec=pltpu.PrefetchScalarGridSpec(
            num_scalar_prefetch=1, grid=grid, in_specs=in_specs, out_specs=out_specs
        ),
        compiler_params=pltpu.CompilerParams(vmem_limit_bytes=vmem * MIB),
        cost_estimate=pl.CostEstimate(flops=cost[0], bytes_accessed=cost[1], transcendentals=0),
    )(scalars, *args)


def whole(shape):
    return pl.BlockSpec(tuple(shape), lambda *_: (0,) * len(shape))


def struct(shape, dtype=BF):
    return jax.ShapeDtypeStruct(tuple(shape), dtype)


def factors(scalars, gate, up):
    blocks, rows, width = gate.shape
    half = blocks // 2

    def kernel(_, gate_ref, up_ref, hidden_ref, silu_ref, slope_ref):
        g = gate_ref[...].astype(F32)
        u = up_ref[...].astype(F32)
        sig = 1.0 / (1.0 + jnp.exp(-g))
        silu = g * sig
        hidden_ref[...] = (silu * u).astype(BF)

        @pl.when(pl.program_id(0) < half)
        def _():
            silu_ref[...] = silu
            slope_ref[...] = u * sig * (1.0 + g * (1.0 - sig))

    block = (1, rows, width)
    pick = pl.BlockSpec(block, lambda i, s: (s[i], 0, 0))
    moved = pl.BlockSpec(block, lambda i, s: (lax.rem(i + s[blocks], blocks), 0, 0))
    mine = pl.BlockSpec(block, lambda i, s: (jnp.minimum(i, half - 1), 0, 0))
    return call(
        kernel, scalars, (gate, up), [pick, pick], [moved, mine, mine],
        [struct(gate.shape), struct((half, rows, width), F32), struct((half, rows, width), F32)],
        (blocks,), (10 * gate.size, 10 * gate.size), 24,
    )


def hidden_part(core, grads, weight, first, width):
    tokens, depth = grads.shape
    half = tokens // 2

    def kernel(core_ref, grads_ref, weight_ref, mine_ref, other_ref):
        total = dot(grads_ref[...], weight_ref[first : first + width], NT)
        is_first = core_ref[0] == 0
        mine_ref[...] = jnp.where(is_first, total[:half], total[half:])
        other_ref[...] = jnp.where(is_first, total[half:], total[:half]).astype(BF)

    return call(
        kernel, core, (grads, weight),
        [pl.BlockSpec(memory_space=pltpu.VMEM), pl.BlockSpec(memory_space=pltpu.VMEM)],
        [pl.BlockSpec(memory_space=pltpu.VMEM), pl.BlockSpec(memory_space=pltpu.VMEM)],
        [struct((half, width), F32), struct((half, width))],
        (), (2 * tokens * depth * width, 2 * depth * width), 40,
    )


def input_part(core, grads, gate_weight, up_weight, first, width, by_halves):
    half = grads[0][0].shape[1]
    units = gate_weight.shape[1]
    block = tile(width, 256, 128)
    n = len(grads)

    def kernel(core_ref, *refs):
        ins, (gate_ref, up_ref), (keep_ref, send_ref) = refs[: 2 * n], refs[2 * n : 2 * n + 2], refs[2 * n + 2 :]
        is_first = core_ref[0] == 0
        total = None
        at = 0
        for k in range(n):
            mine_ref, other_ref = ins[2 * k : 2 * k + 2]
            size = mine_ref.shape[2]
            for which, weight_ref in ((0, gate_ref), (1, up_ref)):
                both = jnp.concatenate([mine_ref[which], other_ref[which]], axis=0)
                part = dot(both, weight_ref[:, at : at + size], NT)
                total = part if total is None else total + part
            at += size
        low = jnp.where(is_first, total[:half], total[half:]).astype(BF)
        high = jnp.where(is_first, total[half:], total[:half]).astype(BF)
        if by_halves:
            keep_ref[0], send_ref[0] = low[: half // 2], low[half // 2 :]
            keep_ref[1], send_ref[1] = high[: half // 2], high[half // 2 :]
        else:
            keep_ref[...], send_ref[...] = low, high

    weight_spec = pl.BlockSpec((block, units), lambda i, core: (first // block + i, 0))
    shape = (2, half // 2, width) if by_halves else (half, width)
    out_block = shape[:-1] + (block,)
    out_spec = pl.BlockSpec(out_block, lambda i, core: (0,) * (len(shape) - 1) + (i,))
    return call(
        kernel, core, [a for pair in grads for a in pair] + [gate_weight, up_weight],
        [whole(a.shape) for pair in grads for a in pair] + [weight_spec, weight_spec],
        [out_spec, out_spec], [struct(shape), struct(shape)],
        (width // block,), (8 * half * units * width, 4 * units * width), 40,
    )


def weight_grads(order, tokens, grads):
    blocks, rows, features = tokens.shape
    half = grads[0][0].shape[1]
    units = sum(mine.shape[2] for mine, _ in grads)
    block = tile(features, 512, 128)
    n = len(grads)

    def kernel(order_ref, tokens_ref, *refs):
        ins, outs = refs[: 2 * n], refs[2 * n :]
        left = jnp.concatenate([tokens_ref[order_ref[i]] for i in range(blocks)], axis=0)
        at = 0
        for k in range(n):
            mine_ref, other_ref = ins[2 * k : 2 * k + 2]
            size = mine_ref.shape[2]
            for which in range(2):
                both = jnp.concatenate([mine_ref[which], other_ref[which]], axis=0)
                outs[which][:, at : at + size] = dot(left, both, TN).astype(BF)
            at += size

    out_spec = pl.BlockSpec((block, units), lambda i, order: (i, 0))
    return call(
        kernel, order, [tokens] + [a for pair in grads for a in pair],
        [pl.BlockSpec((blocks, rows, block), lambda i, order: (0, 0, i))] + [whole(a.shape) for pair in grads for a in pair],
        [out_spec, out_spec], [struct((features, units)), struct((features, units))],
        (features // block,), (8 * half * units * features, 4 * units * features), 48,
    )


def down_grads(hidden, grads):
    tokens, units = hidden.shape
    features = grads.shape[1]
    block = tile(units, 256, 128)

    def kernel(_, hidden_ref, grads_ref, out_ref):
        out_ref[...] = dot(hidden_ref[...], grads_ref[...], TN).astype(BF)

    return call(
        kernel, jnp.zeros((1,), jnp.int32), (hidden, grads),
        [pl.BlockSpec((tokens, block), lambda i, _: (0, i)), whole(grads.shape)],
        pl.BlockSpec((block, features), lambda i, _: (i, 0)), struct((units, features)),
        (units // block,), (2 * tokens * units * features, 2 * units * features), 32,
    )


def on_device(n_row, n_col, tokens, out_grad, gate_saved, up_saved, gate_weight, up_weight, down_weight):
    rows, features = tokens.shape
    units = gate_saved.shape[1]
    row = lax.axis_index("row").astype(jnp.int32)
    core = (lax.axis_index("col") % 2).astype(jnp.int32)
    core_arg = core.reshape(1)

    def swap(x, mask, axis="row"):
        n = n_row if axis == "row" else n_col
        return lax.ppermute(x, axis, [(i, i ^ mask) for i in range(n)])

    masks = []
    m = n_row // 2
    while m > 1:
        masks.append(m)
        m //= 2
    codes = [0]
    for m in masks:
        codes += [i ^ m for i in codes]
    order = jnp.array(codes + [i ^ 1 for i in codes], jnp.int32) ^ row
    order_mine = order ^ core

    held, swapped = [out_grad], [swap(out_grad, 1)]
    for m in masks:
        got = swap(jnp.concatenate(held, axis=0) if len(held) > 1 else held[0], m)
        held.append(got)
        swapped.append(swap(got, 1))
    all_grads = jnp.concatenate(held + swapped, axis=0)

    hidden, silu, slope = factors(
        jnp.concatenate([order_mine, core_arg * (n_row // 2)]),
        gate_saved.reshape(n_row, rows, units), up_saved.reshape(n_row, rows, units),
    )
    hidden = hidden.reshape(n_row * rows, units)
    half = n_row * rows // 2
    silu, slope = silu.reshape(half, units), slope.reshape(half, units)

    all_grads, later = lax.optimization_barrier((all_grads, tokens))
    all_tokens = lax.all_gather(later, "row", axis=0, tiled=True).reshape(n_row, rows, features)

    parts = 2 if (units // 2) % 128 == 0 else 1
    width = units // parts
    partial = [hidden_part(core_arg, all_grads, down_weight, k * width, width) for k in range(parts)]
    grads = []
    for k, (mine, other) in enumerate(partial):
        total = mine + swap(other, 1, "col").astype(F32)
        m = 2
        while m < n_col:
            total = total + swap(total.astype(BF), m, "col").astype(F32)
            m *= 2
        at = slice(k * width, (k + 1) * width)
        pair = jnp.stack([(total * slope[:, at]).astype(BF), (total * silu[:, at]).astype(BF)])
        grads.append((pair, swap(pair, 1, "col")))

    down_grad = down_grads(hidden, all_grads)

    wide = features // 2
    keep, send = input_part(core_arg, grads, gate_weight, up_weight, 0, wide, False)
    keep2, send2 = input_part(core_arg, grads, gate_weight, up_weight, wide, wide, True)
    left = keep + swap(send, 1)
    right = keep2 + swap(send2, masks[-1])
    n = left.shape[0] // 2
    left = left[:n] + swap(left[n:], masks[-1])
    right = right[0] + swap(right[1], 1)
    total = jnp.concatenate([left, right], axis=1)
    for m in masks[-2::-1]:
        n = total.shape[0] // 2
        total = total[:n] + swap(total[n:], m)

    gate_grad, up_grad = weight_grads(order_mine, all_tokens, grads)
    return total, gate_grad, up_grad, down_grad


def solution(mesh):
    n_row, n_col = mesh.shape["row"], mesh.shape["col"]
    return jax.shard_map(
        lambda *args: on_device(n_row, n_col, *args),
        mesh=mesh,
        in_specs=(
            P("row", "col"),
            P("row", "col"),
            P(None, "row"),
            P(None, "row"),
            P("col", "row"),
            P("col", "row"),
            P("row", "col"),
        ),
        out_specs=(P("row", "col"), P("col", "row"), P("col", "row"), P("row", "col")),
        check_vma=False,
    )
```

```python
import jax
import jax.numpy as jnp
from jax import lax
from jax.experimental import pallas as pl
from jax.experimental.pallas import tpu as pltpu
from jax.sharding import PartitionSpec as P

BF = jnp.bfloat16
F32 = jnp.float32
NN = (((1,), (0,)), ((), ()))
NT = (((1,), (1,)), ((), ()))
MIB = 1 << 20
VMEM = pl.BlockSpec(memory_space=pltpu.VMEM)
ANY = pl.BlockSpec(memory_space=pl.ANY)
HBM = pl.BlockSpec(memory_space=pltpu.HBM)
SMEM = pl.BlockSpec(memory_space=pltpu.SMEM)


def dot(a, b, dims):
    return lax.dot_general(a, b, dims, preferred_element_type=F32)


def stack(parts):
    return jnp.concatenate(parts, axis=0) if len(parts) > 1 else parts[0]


def pieces(size, step):
    return [(at, min(step, size - at)) for at in range(0, size, step)]


def struct(shape, dtype=BF):
    return jax.ShapeDtypeStruct(tuple(shape), dtype)


def call(kernel, args, in_specs, out_specs, out_shape, cost, vmem, after=(), aliases=None, scratch=(), mark=False):
    n, m = len(args), len(out_shape)

    def body(*refs):
        outs = refs[n + len(after) :]
        if mark:
            outs[m][...] = jnp.zeros((8, 128), F32)
            outs = outs[:m] + outs[m + 1 :]
        kernel(*refs[:n], *outs)

    out = pl.pallas_call(
        body,
        out_shape=list(out_shape) + [struct((8, 128), F32)] * mark,
        in_specs=list(in_specs) + [ANY] * len(after),
        out_specs=list(out_specs) + [VMEM] * mark,
        scratch_shapes=scratch,
        input_output_aliases=aliases or {},
        compiler_params=pltpu.CompilerParams(vmem_limit_bytes=vmem * MIB),
        cost_estimate=pl.CostEstimate(flops=cost[0], bytes_accessed=cost[1], transcendentals=0),
    )(*args, *after)
    return out if len(out) > 1 else out[0]


def hold(x, after):
    def kernel(x_ref, out_ref):
        out_ref[...] = x_ref[...]

    return call(kernel, (x,), [VMEM], [VMEM], [struct(x.shape, x.dtype)], (0, 4 * x.size), 8, after)


def brought(ranges, vmem, after=()):
    n = len(ranges)

    def kernel(*refs):
        copies = [
            pltpu.make_async_copy(refs[k].at[pl.ds(first, count)], refs[n + k], refs[2 * n].at[k])
            for k, (_, first, count) in enumerate(ranges)
        ]
        for copy in copies:
            copy.start()
        for copy in copies:
            copy.wait()

    return call(
        kernel, [x for x, _, _ in ranges], [HBM] * n, [VMEM] * n, [struct((count, x.shape[1])) for x, _, count in ranges],
        (0, sum(2 * count * x.shape[1] for x, _, count in ranges)), vmem, after,
        scratch=[pltpu.SemaphoreType.DMA((n,))], mark=True,
    )


def factors(order, places, gate, up, after=()):
    blocks, rows, width = gate.shape
    half = blocks // 2

    def kernel(order_ref, places_ref, gate_ref, up_ref, hidden_ref, slope_ref, silu_ref, held, sem):
        copies = []
        for i in range(blocks):
            for k, ref in enumerate((gate_ref, up_ref)):
                copies.append(pltpu.make_async_copy(ref.at[order_ref[i]], held.at[k, i], sem.at[k, i]))
                copies[-1].start()
        for i in range(blocks):
            copies[2 * i].wait()
            copies[2 * i + 1].wait()
            g = held[0, i].astype(F32)
            u = held[1, i].astype(F32)
            sig = 1.0 / (1.0 + jnp.exp(-g))
            silu = g * sig
            hidden_ref[places_ref[i]] = (silu * u).astype(BF)
            if i < half:
                silu_ref[i] = silu
                slope_ref[i] = u * sig * (1.0 + g * (1.0 - sig))

    return call(
        kernel, (order, places, gate, up), [SMEM, SMEM, HBM, HBM], [VMEM] * 3,
        [struct(gate.shape), struct((half, rows, width), F32), struct((half, rows, width), F32)],
        (10 * gate.size, 10 * gate.size), 36, after,
        scratch=[pltpu.VMEM((2, blocks, rows, width), BF), pltpu.SemaphoreType.DMA((2, blocks))],
    )


class Blocks:
    def __init__(self):
        self.arrays, self.place = [], {}

    def add(self, x, codes):
        for i, code in enumerate(codes):
            self.place[code] = (len(self.arrays), i)
        self.arrays.append(x)

    def read(self, refs, codes, columns=slice(None)):
        return stack([refs[self.place[c][0]][self.place[c][1], :, columns] for c in codes])


def hidden_part(core, grads, weight, after=()):
    half, width = grads.shape[0] // 2, weight.shape[0]

    def kernel(core_ref, grads_ref, weight_ref, mine_ref, other_ref):
        total = dot(grads_ref[...], weight_ref[...], NT)
        is_first = core_ref[0] == 0
        mine_ref[...] = jnp.where(is_first, total[:half], total[half:])
        other_ref[...] = jnp.where(is_first, total[half:], total[:half]).astype(BF)

    return call(
        kernel, (core, grads, weight), [SMEM, VMEM, VMEM], [VMEM] * 2, [struct((half, width), F32), struct((half, width))],
        (4 * half * weight.size, 2 * weight.size), 12, after,
    )


def partial_sum(mine, arrived):
    def kernel(mine_ref, arrived_ref, out_ref):
        out_ref[...] = (mine_ref[...] + arrived_ref[...].astype(F32)).astype(BF)

    return call(kernel, (mine, arrived), [VMEM] * 2, [VMEM], [struct(mine.shape)], (mine.size, 8 * mine.size), 8)


def local_grads(mine, arrived, slope, silu, first, after=()):
    rows, width = mine.shape

    def kernel(mine_ref, *refs):
        slope_ref, silu_ref, pair_ref = refs[-3:]
        total = mine_ref[...]
        for ref in refs[:-3]:
            total = total + ref[...].astype(F32)
        pair_ref[0] = (total * slope_ref[:, :, first : first + width].reshape(rows, width)).astype(BF)
        pair_ref[1] = (total * silu_ref[:, :, first : first + width].reshape(rows, width)).astype(BF)

    args = (mine, *arrived, slope, silu)
    return call(
        kernel, args, [VMEM] * len(args), [VMEM], [struct((2, rows, width))], (6 * mine.size, 16 * mine.size), 6, after
    )


def in_order(core, pairs, after=()):
    half = pairs[0][0].shape[1]
    widths = [mine.shape[2] for mine, _ in pairs]
    n = 2 * len(pairs)

    def kernel(core_ref, *refs):
        ins, outs = refs[:n], refs[n:]

        def put(low):
            at = 0
            for k, width in enumerate(widths):
                for which, ref in enumerate(outs):
                    ref[:half, at : at + width] = ins[2 * k + low][which]
                    ref[half:, at : at + width] = ins[2 * k + 1 - low][which]
                at += width

        @pl.when(core_ref[0] == 0)
        def _():
            put(0)

        @pl.when(core_ref[0] != 0)
        def _():
            put(1)

    shape = struct((2 * half, sum(widths)))
    return call(
        kernel, (core, *[x for pair in pairs for x in pair]), [SMEM] + [VMEM] * n, [VMEM] * 2,
        [shape] * 2, (shape.size, 8 * shape.size), 8, after,
    )


def turned(blocks, codes, after=()):
    rows, width = blocks.arrays[0].shape[1:]
    total = rows * len(codes)

    def kernel(*refs):
        ins, out_ref = refs[:-1], refs[-1]
        for at, size in pieces(width, 512):
            out_ref[at : at + size] = blocks.read(ins, codes, slice(at, at + size)).T

    return call(
        kernel, blocks.arrays, [VMEM] * len(blocks.arrays), [VMEM], [struct((width, total))],
        (total * width, 4 * total * width), 6, after,
    )


def input_part(gate, up, weights, first, wide, rows, groups, place, vmem, after=()):
    tokens, units = gate.shape
    shape = (len(groups[0]), len(groups[0][0]), rows, wide)
    cuts = pieces(wide, 512)
    load = first is not None

    def kernel(gate_ref, up_ref, *refs):
        weight_refs, outs = refs[:2], refs[2:4]
        copies = []
        if load:
            held, sem = refs[4:]
            for i, (at, size) in enumerate(cuts):
                for k in (0, 1):
                    copies.append(
                        pltpu.make_async_copy(
                            weight_refs[k].at[pl.ds(first + at, size)], held.at[k, pl.ds(at, size)], sem.at[k, i]
                        )
                    )
            weight_refs = [held.at[0], held.at[1]]
        for copy in copies[:2]:
            copy.start()
        for i, (at, size) in enumerate(cuts):
            total = 0.0
            for k, ref in enumerate((gate_ref, up_ref)):
                if load:
                    copies[2 * i + k].wait()
                    if 2 * i + k + 2 < len(copies):
                        copies[2 * i + k + 2].start()
                total = total + dot(ref[...], weight_refs[k][at : at + size], NT)
            for ref, group in zip(outs, groups):
                for g, codes in enumerate(group):
                    for j, code in enumerate(codes):
                        b = place[code] * rows
                        ref[g, j, :, at : at + size] = total[b : b + rows].astype(BF)

    return call(
        kernel, (gate, up, *weights), [VMEM] * 2 + [HBM if load else VMEM] * 2, [VMEM] * 2, [struct(shape)] * 2,
        (4 * tokens * units * wide, 4 * units * wide), vmem, after,
        scratch=[pltpu.VMEM((2, wide, units), BF), pltpu.SemaphoreType.DMA((2, len(cuts)))] if load else (), mark=True,
    )


def fold(keep, arrived, after=()):
    def kernel(keep_ref, arrived_ref, a_ref, b_ref):
        a_ref[...] = keep_ref[0] + arrived_ref[0]
        b_ref[...] = keep_ref[1] + arrived_ref[1]

    shape = struct(keep.shape[1:])
    return call(kernel, (keep, arrived), [VMEM] * 2, [VMEM] * 2, [shape, shape], (keep.size, 6 * keep.size), 8, after)


def join(left, left_arrived, right, right_arrived, after=()):
    blocks, rows, wide = left.shape
    half = blocks // 2

    def kernel(a_ref, b_ref, c_ref, d_ref, *outs):
        for k, ref in enumerate(outs):
            at = slice(k * half, (k + 1) * half) if half else slice(None)
            ref[:, :, :wide] = a_ref[at] + b_ref[at]
            ref[:, :, wide:] = c_ref[at] + d_ref[at]

    shape = struct((half or blocks, rows, 2 * wide))
    out = call(
        kernel, (left, left_arrived, right, right_arrived), [VMEM] * 4, [VMEM] * (2 if half else 1),
        [shape] * (2 if half else 1), (left.size * 2, 12 * left.size), 8, after,
    )
    return out if half else (out, None)


def long_product(left, right, begin, end, into=None, after=(), ahead=None, step=512, vmem=24):
    height, depth = left.shape
    width = right.shape[1]
    cuts = [(begin + at, size) for at, size in pieces(end - begin, step)]
    slots = 2
    ahead = ahead or []
    n = len(ahead)
    m = 0 if into is None else 1

    def kernel(left_ref, right_ref, *refs):
        sources, (out_ref, *targets), (held, sem, *more) = refs[:n], refs[n + m : 2 * n + m + 1], refs[2 * n + m + 1 :]
        early = [
            pltpu.make_async_copy(a.at[pl.ds(first, count)], b, more[0].at[k])
            for k, (a, b, (_, first, count)) in enumerate(zip(sources, targets, ahead))
        ]
        for copy in early:
            copy.start()
        copies = []
        for i, (at, size) in enumerate(cuts):
            value = dot(left_ref[at : at + size], right_ref[...], NN).astype(BF)
            if i >= slots:
                copies[i - slots].wait()
            held[i % slots, :size] = value
            copies.append(
                pltpu.make_async_copy(held.at[i % slots, pl.ds(0, size)], out_ref.at[pl.ds(at, size)], sem.at[i % slots])
            )
            copies[-1].start()
        for copy in copies[-slots:] + early:
            copy.wait()

    args = [left, right] + [x for x, _, _ in ahead] + ([into] if m else [])
    return call(
        kernel, args, [VMEM] * 2 + [HBM] * (n + m), [HBM] + [VMEM] * n,
        [struct((height, width))] + [struct((count, x.shape[1])) for x, _, count in ahead],
        (2 * depth * width * (end - begin), 2 * width * (end - begin)), vmem, after, {len(args) - 1: 0} if m else None,
        scratch=[pltpu.VMEM((slots, step, width), BF), pltpu.SemaphoreType.DMA((slots,))]
        + ([pltpu.SemaphoreType.DMA((n,))] if n else []),
        mark=True,
    )


def laid(parts):
    if len(parts) == 1:
        return parts[0]

    def kernel(*refs):
        at = 0
        for ref in refs[:-1]:
            refs[-1][at : at + ref.shape[0]] = ref[...]
            at += ref.shape[0]

    count = sum(x.shape[0] for x in parts)
    return call(
        kernel, parts, [VMEM] * len(parts), [VMEM], [struct((count, *parts[0].shape[1:]))], (0, 4 * count * parts[0].size), 8
    )


def stacked(blocks, codes, after=()):
    rows, width = blocks.arrays[0].shape[1:]
    total = rows * len(codes)

    def kernel(*refs):
        refs[-1][...] = blocks.read(refs[:-1], codes)

    return call(
        kernel, blocks.arrays, [VMEM] * len(blocks.arrays), [VMEM], [struct((total, width))],
        (total * width, 4 * total * width), 8, after,
    )


def on_device(n_row, n_col, tokens, out_grad, gate_saved, up_saved, gate_weight, up_weight, down_weight):
    rows, features = tokens.shape
    units = gate_saved.shape[1]
    row = lax.axis_index("row").astype(jnp.int32)
    core_index = (lax.axis_index("col") % 2).astype(jnp.int32)
    core = core_index.reshape(1)

    def swap(x, mask, axis="row"):
        n = n_row if axis == "row" else n_col
        return lax.ppermute(x, axis, [(i, i ^ mask) for i in range(n)])

    def closure(masks):
        codes = [0]
        for m in masks:
            codes += [c ^ m for c in codes]
        return codes

    def move(codes, mask):
        return [c ^ mask for c in codes]

    masks = [m for m in (1 << i for i in range(1, 31)) if m < n_row]
    low = closure(masks)
    codes = low + move(low, 1)
    place = {c: i for i, c in enumerate(codes)}
    q = len(low)
    order = jnp.array(codes, jnp.int32) ^ row ^ core_index
    places = jnp.arange(2 * q, dtype=jnp.int32) ^ (core_index * q)

    own = out_grad.reshape(1, rows, features)
    held = [(own, [0])]
    for m in masks[:0:-1]:
        held.append((swap(stack([x for x, _ in held]), m), [c ^ m for _, cs in held for c in cs]))
    near = [(swap(held[0][0], masks[0]), move(held[0][1], masks[0]))]
    parts = 2 if (units // 2) % 128 == 0 else 1
    width = units // parts
    *weight_rows, mark = brought([(down_weight, k * width, width) for k in range(parts)], 34, (order, places))
    held = held[:1] + [(hold(x, (mark, near[0][0])), cs) for x, cs in held[1:]]
    near += [(swap(x, masks[0]), move(cs, masks[0])) for x, cs in held[1:]]
    held += near
    grads = Blocks()
    for x, cs in held + [(swap(x, 1), move(cs, 1)) for x, cs in held]:
        grads.add(x, cs)
    all_grads = stacked(grads, codes)

    def summed(mine, other):
        arrived = [swap(other, 1, "col")]
        sent, m = None, 2
        while m < n_col:
            if len(arrived) > 1:
                mine = mine + arrived.pop(0).astype(F32)
            sent = partial_sum(mine, arrived[-1])
            arrived.append(swap(sent, m, "col"))
            m *= 2
        return mine, arrived, sent

    sums = []
    for k in range(parts):
        after = (sums[-1][1],) if k else ()
        sums.append(hidden_part(core, all_grads, weight_rows[k], after))
    sums = [summed(*x) for x in sums]

    all_tokens = Blocks()
    held = [(hold(tokens.reshape(1, rows, features), (sums[-1][2],)), [0])]
    for m in masks[::-1]:
        joined = laid([x for x, _ in held])
        held.append((swap(joined, m), [c ^ m for _, cs in held for c in cs]))
    base_crossed = swap(joined, 1)
    crossed = [(base_crossed, [c ^ 1 for _, cs in held[:-1] for c in cs]), (swap(held[-1][0], 1), move(held[-1][1], 1))]
    for x, cs in held + crossed:
        all_tokens.add(x, cs)

    hidden, slope, silu = factors(
        order, places, gate_saved.reshape(n_row, rows, units), up_saved.reshape(n_row, rows, units), (sums[0][2],)
    )
    hidden_blocks = Blocks()
    hidden_blocks.add(hidden, codes)
    hidden_turned = turned(hidden_blocks, codes)
    wide = features // 2
    weights = (gate_weight, up_weight)
    down_grad, a, b, c, d, mark = long_product(
        hidden_turned, all_grads, 0, units, None, (sums[-1][2],),
        [(x, at, wide) for at in (0, wide) for x in weights], 256, 12,
    )
    left_weights, right_weights = (a, b), (c, d)
    pairs = []
    for k, (mine, arrived, _) in enumerate(sums):
        after = (mark, base_crossed, held[-1][0])
        pairs.append(local_grads(mine, arrived, slope, silu, k * width, after))
    gate, up = in_order(core, [(pair, swap(pair, 1, "col")) for pair in pairs])
    tokens_turned = turned(all_tokens, codes)

    rest = closure(masks[1:])
    m = masks[0]
    *left, mark = input_part(
        gate, up, left_weights, None, wide, rows, [[rest, move(rest, m)], [move(rest, 1), move(rest, 1 ^ m)]], place, 7
    )
    *right, mark = input_part(
        gate, up, right_weights, None, wide, rows, [[rest, move(rest, 1)], [move(rest, m), move(rest, m ^ 1)]], place, 7, (mark,)
    )
    cut = features // 2 // 512 * 512
    left_got, right_got = swap(left[1], 1), swap(right[1], m)
    left = fold(left[0], left_got)
    left_got = swap(left[1], m)
    gate_grad, mark = long_product(tokens_turned, gate, 0, cut, None, (left[1],))
    right = fold(right[0], right_got, (mark,))
    right_got = swap(right[1], 1)
    gate_grad, mark = long_product(tokens_turned, gate, cut, features, gate_grad, (left_got, right[1]))
    total, sent = join(left[0], left_got, right[0], right_got, (mark,))
    for k, m in enumerate(masks[:0:-1]):
        if k > 0:
            n = total.shape[0] // 2
            total, sent = total[:n], total[n:]
        got = swap(sent, m)
        if k == 0:
            up_grad, _ = long_product(tokens_turned, up, 0, features, None, (sent,))
        total = total + got
    return total.reshape(rows, features), gate_grad, up_grad, down_grad


def solution(mesh):
    n_row, n_col = mesh.shape["row"], mesh.shape["col"]
    return jax.shard_map(
        lambda *args: on_device(n_row, n_col, *args),
        mesh=mesh,
        in_specs=(
            P("row", "col"),
            P("row", "col"),
            P(None, "row"),
            P(None, "row"),
            P("col", "row"),
            P("col", "row"),
            P("row", "col"),
        ),
        out_specs=(P("row", "col"), P("col", "row"), P("col", "row"), P("row", "col")),
        check_vma=False,
    )
```

```python
import jax
import jax.numpy as jnp
from jax import lax
from jax.experimental import pallas as pl
from jax.experimental.pallas import tpu as pltpu
from jax.sharding import PartitionSpec as P

BF = jnp.bfloat16
F32 = jnp.float32
NN = (((1,), (0,)), ((), ()))
NT = (((1,), (1,)), ((), ()))
MIB = 1 << 20
VMEM = pl.BlockSpec(memory_space=pltpu.VMEM)
ANY = pl.BlockSpec(memory_space=pl.ANY)
HBM = pl.BlockSpec(memory_space=pltpu.HBM)
SMEM = pl.BlockSpec(memory_space=pltpu.SMEM)


def dot(a, b, dims):
    return lax.dot_general(a, b, dims, preferred_element_type=F32)


def stack(parts):
    return jnp.concatenate(parts, axis=0) if len(parts) > 1 else parts[0]


def pieces(size, step):
    return [(at, min(step, size - at)) for at in range(0, size, step)]


def struct(shape, dtype=BF):
    return jax.ShapeDtypeStruct(tuple(shape), dtype)


def call(kernel, args, in_specs, out_specs, out_shape, cost, vmem, after=(), aliases=None, scratch=(), mark=False):
    n, m = len(args), len(out_shape)

    def body(*refs):
        outs = refs[n + len(after) :]
        if mark:
            outs[m][...] = jnp.zeros((8, 128), F32)
            outs = outs[:m] + outs[m + 1 :]
        kernel(*refs[:n], *outs)

    out = pl.pallas_call(
        body,
        out_shape=list(out_shape) + [struct((8, 128), F32)] * mark,
        in_specs=list(in_specs) + [ANY] * len(after),
        out_specs=list(out_specs) + [VMEM] * mark,
        scratch_shapes=scratch,
        input_output_aliases=aliases or {},
        compiler_params=pltpu.CompilerParams(vmem_limit_bytes=vmem * MIB),
        cost_estimate=pl.CostEstimate(flops=cost[0], bytes_accessed=cost[1], transcendentals=0),
    )(*args, *after)
    return out if len(out) > 1 else out[0]


def hold(x, after):
    def kernel(x_ref, out_ref):
        out_ref[...] = x_ref[...]

    return call(kernel, (x,), [VMEM], [VMEM], [struct(x.shape, x.dtype)], (0, 4 * x.size), 8, after)


def brought(ranges, vmem, after=()):
    n = len(ranges)

    def kernel(*refs):
        copies = [
            pltpu.make_async_copy(refs[k].at[pl.ds(first, count)], refs[n + k], refs[2 * n].at[k])
            for k, (_, first, count) in enumerate(ranges)
        ]
        for copy in copies:
            copy.start()
        for copy in copies:
            copy.wait()

    return call(
        kernel, [x for x, _, _ in ranges], [HBM] * n, [VMEM] * n, [struct((count, x.shape[1])) for x, _, count in ranges],
        (0, sum(2 * count * x.shape[1] for x, _, count in ranges)), vmem, after,
        scratch=[pltpu.SemaphoreType.DMA((n,))], mark=True,
    )


def factors(order, places, gate, up, after=()):
    blocks, rows, width = gate.shape
    half = blocks // 2

    def kernel(order_ref, places_ref, gate_ref, up_ref, turned_ref, slope_ref, silu_ref, held, hidden_ref, sem):
        copies = []
        for i in range(blocks):
            for k, ref in enumerate((gate_ref, up_ref)):
                copies.append(pltpu.make_async_copy(ref.at[order_ref[i]], held.at[k, i], sem.at[k, i]))
                copies[-1].start()
        for i in range(blocks):
            copies[2 * i].wait()
            copies[2 * i + 1].wait()
            g = held[0, i].astype(F32)
            u = held[1, i].astype(F32)
            sig = 1.0 / (1.0 + jnp.exp(-g))
            silu = g * sig
            hidden_ref[places_ref[i]] = (silu * u).astype(BF)
            if i < half:
                silu_ref[i] = silu
                slope_ref[i] = u * sig * (1.0 + g * (1.0 - sig))
        for at, size in pieces(width, 512):
            turned_ref[at : at + size] = stack([hidden_ref[i, :, at : at + size] for i in range(blocks)]).T

    return call(
        kernel, (order, places, gate, up), [SMEM, SMEM, HBM, HBM], [VMEM] * 3,
        [struct((width, blocks * rows)), struct((half, rows, width), F32), struct((half, rows, width), F32)],
        (10 * gate.size, 10 * gate.size), 20, after,
        scratch=[pltpu.VMEM((2, blocks, rows, width), BF), pltpu.VMEM(gate.shape, BF), pltpu.SemaphoreType.DMA((2, blocks))],
    )


class Blocks:
    def __init__(self):
        self.arrays, self.place = [], {}

    def add(self, x, codes):
        for i, code in enumerate(codes):
            self.place[code] = (len(self.arrays), i)
        self.arrays.append(x)

    def read(self, refs, codes, columns=slice(None)):
        return stack([refs[self.place[c][0]][self.place[c][1], :, columns] for c in codes])


def hidden_part(core, grads, weight, after=()):
    half, width = grads.shape[0] // 2, weight.shape[0]

    def kernel(core_ref, grads_ref, weight_ref, mine_ref, other_ref):
        total = dot(grads_ref[...], weight_ref[...], NT)
        is_first = core_ref[0] == 0
        mine_ref[...] = jnp.where(is_first, total[:half], total[half:])
        other_ref[...] = jnp.where(is_first, total[half:], total[:half]).astype(BF)

    return call(
        kernel, (core, grads, weight), [SMEM, VMEM, VMEM], [VMEM] * 2, [struct((half, width), F32), struct((half, width))],
        (4 * half * weight.size, 2 * weight.size), 12, after,
    )


def partial_sum(mine, arrived, after=()):
    def kernel(mine_ref, arrived_ref, out_ref):
        out_ref[...] = (mine_ref[...] + arrived_ref[...].astype(F32)).astype(BF)

    return call(kernel, (mine, arrived), [VMEM] * 2, [VMEM], [struct(mine.shape)], (mine.size, 8 * mine.size), 8, after)


def local_grads(mine, arrived, slope, silu, first, after=()):
    rows, width = mine.shape

    def kernel(mine_ref, *refs):
        slope_ref, silu_ref, pair_ref = refs[-3:]
        total = mine_ref[...]
        for ref in refs[:-3]:
            total = total + ref[...].astype(F32)
        pair_ref[0] = (total * slope_ref[:, :, first : first + width].reshape(rows, width)).astype(BF)
        pair_ref[1] = (total * silu_ref[:, :, first : first + width].reshape(rows, width)).astype(BF)

    args = (mine, *arrived, slope, silu)
    return call(
        kernel, args, [VMEM] * len(args), [VMEM], [struct((2, rows, width))], (6 * mine.size, 16 * mine.size), 6, after
    )


def in_order(core, pairs, after=()):
    half = pairs[0][0].shape[1]
    widths = [mine.shape[2] for mine, _ in pairs]
    n = 2 * len(pairs)

    def kernel(core_ref, *refs):
        ins, outs = refs[:n], refs[n:]

        def put(low):
            at = 0
            for k, width in enumerate(widths):
                for which, ref in enumerate(outs):
                    ref[:half, at : at + width] = ins[2 * k + low][which]
                    ref[half:, at : at + width] = ins[2 * k + 1 - low][which]
                at += width

        @pl.when(core_ref[0] == 0)
        def _():
            put(0)

        @pl.when(core_ref[0] != 0)
        def _():
            put(1)

    shape = struct((2 * half, sum(widths)))
    return call(
        kernel, (core, *[x for pair in pairs for x in pair]), [SMEM] + [VMEM] * n, [VMEM] * 2,
        [shape] * 2, (shape.size, 8 * shape.size), 8, after,
    )


def turned(blocks, codes, after=()):
    rows, width = blocks.arrays[0].shape[1:]
    total = rows * len(codes)

    def kernel(*refs):
        ins, out_ref = refs[:-1], refs[-1]
        for at, size in pieces(width, 512):
            out_ref[at : at + size] = blocks.read(ins, codes, slice(at, at + size)).T

    return call(
        kernel, blocks.arrays, [VMEM] * len(blocks.arrays), [VMEM], [struct((width, total))],
        (total * width, 4 * total * width), 6, after,
    )


def input_part(gate, up, weights, first, wide, rows, groups, place, vmem, after=()):
    tokens, units = gate.shape
    shape = (len(groups[0]), len(groups[0][0]), rows, wide)
    cuts = pieces(wide, 512)
    load = first is not None

    def kernel(gate_ref, up_ref, *refs):
        weight_refs, outs = refs[:2], refs[2:4]
        copies = []
        if load:
            held, sem = refs[4:]
            for i, (at, size) in enumerate(cuts):
                for k in (0, 1):
                    copies.append(
                        pltpu.make_async_copy(
                            weight_refs[k].at[pl.ds(first + at, size)], held.at[k, pl.ds(at, size)], sem.at[k, i]
                        )
                    )
            weight_refs = [held.at[0], held.at[1]]
        for copy in copies[:2]:
            copy.start()
        for i, (at, size) in enumerate(cuts):
            total = 0.0
            for k, ref in enumerate((gate_ref, up_ref)):
                if load:
                    copies[2 * i + k].wait()
                    if 2 * i + k + 2 < len(copies):
                        copies[2 * i + k + 2].start()
                total = total + dot(ref[...], weight_refs[k][at : at + size], NT)
            for ref, group in zip(outs, groups):
                for g, codes in enumerate(group):
                    for j, code in enumerate(codes):
                        b = place[code] * rows
                        ref[g, j, :, at : at + size] = total[b : b + rows].astype(BF)

    return call(
        kernel, (gate, up, *weights), [VMEM] * 2 + [HBM if load else VMEM] * 2, [VMEM] * 2, [struct(shape)] * 2,
        (4 * tokens * units * wide, 4 * units * wide), vmem, after,
        scratch=[pltpu.VMEM((2, wide, units), BF), pltpu.SemaphoreType.DMA((2, len(cuts)))] if load else (), mark=True,
    )


def fold(keep, arrived, after=()):
    def kernel(keep_ref, arrived_ref, a_ref, b_ref):
        a_ref[...] = keep_ref[0] + arrived_ref[0]
        b_ref[...] = keep_ref[1] + arrived_ref[1]

    shape = struct(keep.shape[1:])
    return call(kernel, (keep, arrived), [VMEM] * 2, [VMEM] * 2, [shape, shape], (keep.size, 6 * keep.size), 8, after)


def join(left, left_arrived, right, right_arrived, after=()):
    blocks, rows, wide = left.shape
    half = blocks // 2

    def kernel(a_ref, b_ref, c_ref, d_ref, *outs):
        for k, ref in enumerate(outs):
            at = slice(k * half, (k + 1) * half) if half else slice(None)
            ref[:, :, :wide] = a_ref[at] + b_ref[at]
            ref[:, :, wide:] = c_ref[at] + d_ref[at]

    shape = struct((half or blocks, rows, 2 * wide))
    out = call(
        kernel, (left, left_arrived, right, right_arrived), [VMEM] * 4, [VMEM] * (2 if half else 1),
        [shape] * (2 if half else 1), (left.size * 2, 12 * left.size), 8, after,
    )
    return out if half else (out, None)


def long_product(left, right, begin, end, into=None, after=(), ahead=None, slots=16, vmem=32):
    height, depth = left.shape
    width = right.shape[1]
    cuts = [(begin + at, size) for at, size in pieces(end - begin, 256)]
    slots = min(slots, len(cuts))
    ahead = ahead or []
    n = len(ahead)
    m = 0 if into is None else 1

    def kernel(left_ref, right_ref, *refs):
        sources, (out_ref, *targets), (held, sem, *more) = refs[:n], refs[n + m : 2 * n + m + 1], refs[2 * n + m + 1 :]
        early = [
            pltpu.make_async_copy(a.at[pl.ds(first, count)], b, more[0].at[k])
            for k, (a, b, (_, first, count)) in enumerate(zip(sources, targets, ahead))
        ]
        for copy in early:
            copy.start()
        copies = []
        for i, (at, size) in enumerate(cuts):
            value = dot(left_ref[at : at + size], right_ref[...], NN).astype(BF)
            if i >= slots:
                copies[i - slots].wait()
            held[i % slots, :size] = value
            copies.append(
                pltpu.make_async_copy(held.at[i % slots, pl.ds(0, size)], out_ref.at[pl.ds(at, size)], sem.at[i % slots])
            )
            copies[-1].start()
        for copy in copies[-slots:] + early:
            copy.wait()

    args = [left, right] + [x for x, _, _ in ahead] + ([into] if m else [])
    return call(
        kernel, args, [VMEM] * 2 + [HBM] * (n + m), [HBM] + [VMEM] * n,
        [struct((height, width))] + [struct((count, x.shape[1])) for x, _, count in ahead],
        (2 * depth * width * (end - begin), 2 * width * (end - begin)), vmem, after, {len(args) - 1: 0} if m else None,
        scratch=[pltpu.VMEM((slots, 256, width), BF), pltpu.SemaphoreType.DMA((slots,))]
        + ([pltpu.SemaphoreType.DMA((n,))] if n else []),
        mark=True,
    )


def laid(parts):
    if len(parts) == 1:
        return parts[0]

    def kernel(*refs):
        at = 0
        for ref in refs[:-1]:
            refs[-1][at : at + ref.shape[0]] = ref[...]
            at += ref.shape[0]

    count = sum(x.shape[0] for x in parts)
    return call(
        kernel, parts, [VMEM] * len(parts), [VMEM], [struct((count, *parts[0].shape[1:]))], (0, 4 * count * parts[0].size), 8
    )


def stacked(blocks, codes, after=()):
    rows, width = blocks.arrays[0].shape[1:]
    total = rows * len(codes)

    def kernel(*refs):
        refs[-1][...] = blocks.read(refs[:-1], codes)

    return call(
        kernel, blocks.arrays, [VMEM] * len(blocks.arrays), [VMEM], [struct((total, width))],
        (total * width, 4 * total * width), 8, after,
    )


def on_device(n_row, n_col, tokens, out_grad, gate_saved, up_saved, gate_weight, up_weight, down_weight):
    rows, features = tokens.shape
    units = gate_saved.shape[1]
    row = lax.axis_index("row").astype(jnp.int32)
    core_index = (lax.axis_index("col") % 2).astype(jnp.int32)
    core = core_index.reshape(1)

    def swap(x, mask, axis="row"):
        n = n_row if axis == "row" else n_col
        return lax.ppermute(x, axis, [(i, i ^ mask) for i in range(n)])

    def closure(masks):
        codes = [0]
        for m in masks:
            codes += [c ^ m for c in codes]
        return codes

    def move(codes, mask):
        return [c ^ mask for c in codes]

    masks = [m for m in (1 << i for i in range(1, 31)) if m < n_row]
    low = closure(masks)
    codes = low + move(low, 1)
    place = {c: i for i, c in enumerate(codes)}
    q = len(low)
    order = jnp.array(codes, jnp.int32) ^ row ^ core_index
    places = jnp.arange(2 * q, dtype=jnp.int32) ^ (core_index * q)

    own = out_grad.reshape(1, rows, features)
    held = [(own, [0])]
    for m in masks[:0:-1]:
        held.append((swap(stack([x for x, _ in held]), m), [c ^ m for _, cs in held for c in cs]))
    crossed = swap(own, 1)
    near = [(swap(held[0][0], masks[0]), move(held[0][1], masks[0]))]
    parts = 2 if (units // 2) % 128 == 0 else 1
    width = units // parts
    *weight_rows, mark = brought([(down_weight, k * width, width) for k in range(parts)], 34, (order, places))
    held = held[:1] + [(hold(x, (mark, near[0][0], crossed)), cs) for x, cs in held[1:]]
    near += [(swap(x, masks[0]), move(cs, masks[0])) for x, cs in held[1:]]
    held += near
    grads = Blocks()
    for x, cs in held + [(crossed, [1])] + [(swap(x, 1), move(cs, 1)) for x, cs in held[1:]]:
        grads.add(x, cs)
    hidden_turned, slope, silu = factors(
        order, places, gate_saved.reshape(n_row, rows, units), up_saved.reshape(n_row, rows, units), (near[-1][0],)
    )
    all_grads = stacked(grads, codes, (hidden_turned,))

    all_tokens = Blocks()
    held = [(hold(tokens.reshape(1, rows, features), (near[-1][0],)), [0])]
    for m in masks[::-1]:
        joined = laid([x for x, _ in held])
        held.append((swap(joined, m), [c ^ m for _, cs in held for c in cs]))
    base_crossed = swap(joined, 1)
    crossed = [(base_crossed, [c ^ 1 for _, cs in held[:-1] for c in cs]), (swap(held[-1][0], 1), move(held[-1][1], 1))]
    for x, cs in held + crossed:
        all_tokens.add(x, cs)

    def summed(mine, other, after):
        arrived = [swap(other, 1, "col")]
        sent, m = None, 2
        while m < n_col:
            if len(arrived) > 1:
                mine = mine + arrived.pop(0).astype(F32)
            sent = partial_sum(mine, arrived[-1], after)
            arrived.append(swap(sent, m, "col"))
            m *= 2
        return mine, arrived, sent

    sums, after = [], ()
    for k in range(parts):
        sums.append(hidden_part(core, all_grads, weight_rows[k], after))
        after = (sums[-1][1], all_tokens.arrays[1])
    after = ()
    for k in range(parts):
        sums[k] = summed(*sums[k], after)
        after = (sums[k][2],)

    wide = features // 2
    weights = (gate_weight, up_weight)
    down_grad, a, b, c, d, mark = long_product(
        hidden_turned, all_grads, 0, units, None, (sums[-1][2],),
        [(x, at, wide) for at in (0, wide) for x in weights], 4, 12,
    )
    left_weights, right_weights = (a, b), (c, d)
    pairs = []
    for k, (mine, arrived, _) in enumerate(sums):
        after = (mark, base_crossed, held[-1][0])
        pairs.append(local_grads(mine, arrived, slope, silu, k * width, after))
    gate, up = in_order(core, [(pair, swap(pair, 1, "col")) for pair in pairs])
    tokens_turned = turned(all_tokens, codes)

    rest = closure(masks[1:])
    m = masks[0]
    *left, mark = input_part(
        gate, up, left_weights, None, wide, rows, [[rest, move(rest, m)], [move(rest, 1), move(rest, 1 ^ m)]], place, 7
    )
    *right, mark = input_part(
        gate, up, right_weights, None, wide, rows, [[rest, move(rest, 1)], [move(rest, m), move(rest, m ^ 1)]], place, 7, (mark,)
    )
    cut = features // 2 // 512 * 512
    left_got, right_got = swap(left[1], 1), swap(right[1], m)
    gate_grad, mark = long_product(tokens_turned, gate, 0, cut, None, (mark,))
    left = fold(left[0], left_got, (mark,))
    left_got = swap(left[1], m)
    right = fold(right[0], right_got, (mark,))
    right_got = swap(right[1], 1)
    gate_grad, mark = long_product(tokens_turned, gate, cut, features, gate_grad, (left[1], right[1]))
    total, sent = join(left[0], left_got, right[0], right_got, (mark,))
    for k, m in enumerate(masks[:0:-1]):
        if k > 0:
            n = total.shape[0] // 2
            total, sent = total[:n], total[n:]
        got = swap(sent, m)
        if k == 0:
            up_grad, _ = long_product(tokens_turned, up, 0, features, None, (sent,))
        total = total + got
    return total.reshape(rows, features), gate_grad, up_grad, down_grad


def solution(mesh):
    n_row, n_col = mesh.shape["row"], mesh.shape["col"]
    return jax.shard_map(
        lambda *args: on_device(n_row, n_col, *args),
        mesh=mesh,
        in_specs=(
            P("row", "col"),
            P("row", "col"),
            P(None, "row"),
            P(None, "row"),
            P("col", "row"),
            P("col", "row"),
            P("row", "col"),
        ),
        out_specs=(P("row", "col"), P("col", "row"), P("col", "row"), P("row", "col")),
        check_vma=False,
    )
```

```python
import jax
import jax.numpy as jnp
from jax import lax
from jax.experimental import pallas as pl
from jax.experimental.pallas import tpu as pltpu
from jax.sharding import PartitionSpec as P

BF = jnp.bfloat16
F32 = jnp.float32
NN = (((1,), (0,)), ((), ()))
NT = (((1,), (1,)), ((), ()))
MIB = 1 << 20
VMEM = pl.BlockSpec(memory_space=pltpu.VMEM)
ANY = pl.BlockSpec(memory_space=pl.ANY)
HBM = pl.BlockSpec(memory_space=pltpu.HBM)
SMEM = pl.BlockSpec(memory_space=pltpu.SMEM)


def dot(a, b, dims):
    return lax.dot_general(a, b, dims, preferred_element_type=F32)


def stack(parts):
    return jnp.concatenate(parts, axis=0) if len(parts) > 1 else parts[0]


def pieces(size, step):
    return [(at, min(step, size - at)) for at in range(0, size, step)]


def struct(shape, dtype=BF):
    return jax.ShapeDtypeStruct(tuple(shape), dtype)


def call(kernel, args, in_specs, out_specs, out_shape, cost, vmem, after=(), aliases=None, scratch=(), mark=False):
    n, m = len(args), len(out_shape)

    def body(*refs):
        outs = refs[n + len(after) :]
        if mark:
            outs[m][...] = jnp.zeros((8, 128), F32)
            outs = outs[:m] + outs[m + 1 :]
        kernel(*refs[:n], *outs)

    out = pl.pallas_call(
        body,
        out_shape=list(out_shape) + [struct((8, 128), F32)] * mark,
        in_specs=list(in_specs) + [ANY] * len(after),
        out_specs=list(out_specs) + [VMEM] * mark,
        scratch_shapes=scratch,
        input_output_aliases=aliases or {},
        compiler_params=pltpu.CompilerParams(vmem_limit_bytes=vmem * MIB),
        cost_estimate=pl.CostEstimate(flops=cost[0], bytes_accessed=cost[1], transcendentals=0),
    )(*args, *after)
    return out if len(out) > 1 else out[0]


def hold(x, after):
    def kernel(x_ref, out_ref):
        out_ref[...] = x_ref[...]

    return call(kernel, (x,), [VMEM], [VMEM], [struct(x.shape, x.dtype)], (0, 4 * x.size), 8, after)


def brought(ranges, vmem, after=()):
    n = len(ranges)

    def kernel(*refs):
        copies = [
            pltpu.make_async_copy(refs[k].at[pl.ds(first, count)], refs[n + k], refs[2 * n].at[k])
            for k, (_, first, count) in enumerate(ranges)
        ]
        for copy in copies:
            copy.start()
        for copy in copies:
            copy.wait()

    return call(
        kernel, [x for x, _, _ in ranges], [HBM] * n, [VMEM] * n, [struct((count, x.shape[1])) for x, _, count in ranges],
        (0, sum(2 * count * x.shape[1] for x, _, count in ranges)), vmem, after,
        scratch=[pltpu.SemaphoreType.DMA((n,))], mark=True,
    )


def factors(order, places, gate, up, after=()):
    blocks, rows, width = gate.shape
    half = blocks // 2

    def kernel(order_ref, places_ref, gate_ref, up_ref, turned_ref, slope_ref, silu_ref, held, hidden_ref, sem):
        copies = []
        for i in range(blocks):
            for k, ref in enumerate((gate_ref, up_ref)):
                copies.append(pltpu.make_async_copy(ref.at[order_ref[i]], held.at[k, i], sem.at[k, i]))
                copies[-1].start()
        for i in range(blocks):
            copies[2 * i].wait()
            copies[2 * i + 1].wait()
            g = held[0, i].astype(F32)
            u = held[1, i].astype(F32)
            sig = 1.0 / (1.0 + jnp.exp(-g))
            silu = g * sig
            hidden_ref[places_ref[i]] = (silu * u).astype(BF)
            if i < half:
                silu_ref[i] = silu
                slope_ref[i] = u * sig * (1.0 + g * (1.0 - sig))
        for at, size in pieces(width, 512):
            turned_ref[at : at + size] = stack([hidden_ref[i, :, at : at + size] for i in range(blocks)]).T

    return call(
        kernel, (order, places, gate, up), [SMEM, SMEM, HBM, HBM], [VMEM] * 3,
        [struct((width, blocks * rows)), struct((half, rows, width), F32), struct((half, rows, width), F32)],
        (10 * gate.size, 10 * gate.size), 20, after,
        scratch=[pltpu.VMEM((2, blocks, rows, width), BF), pltpu.VMEM(gate.shape, BF), pltpu.SemaphoreType.DMA((2, blocks))],
    )


class Blocks:
    def __init__(self):
        self.arrays, self.place = [], {}

    def add(self, x, codes):
        for i, code in enumerate(codes):
            self.place[code] = (len(self.arrays), i)
        self.arrays.append(x)

    def read(self, refs, codes, columns=slice(None)):
        return stack([refs[self.place[c][0]][self.place[c][1], :, columns] for c in codes])


def hidden_part(core, grads, weight, after=()):
    half, width = grads.shape[0] // 2, weight.shape[0]

    def kernel(core_ref, grads_ref, weight_ref, mine_ref, other_ref):
        total = dot(grads_ref[...], weight_ref[...], NT)
        is_first = core_ref[0] == 0
        mine_ref[...] = jnp.where(is_first, total[:half], total[half:])
        other_ref[...] = jnp.where(is_first, total[half:], total[:half]).astype(BF)

    return call(
        kernel, (core, grads, weight), [SMEM, VMEM, VMEM], [VMEM] * 2, [struct((half, width), F32), struct((half, width))],
        (4 * half * weight.size, 2 * weight.size), 12, after,
    )


def partial_sum(mine, arrived, after=()):
    def kernel(mine_ref, arrived_ref, out_ref):
        out_ref[...] = (mine_ref[...] + arrived_ref[...].astype(F32)).astype(BF)

    return call(kernel, (mine, arrived), [VMEM] * 2, [VMEM], [struct(mine.shape)], (mine.size, 8 * mine.size), 8, after)


def local_grads(mine, arrived, slope, silu, first, after=()):
    rows, width = mine.shape

    def kernel(mine_ref, *refs):
        slope_ref, silu_ref, pair_ref = refs[-3:]
        total = mine_ref[...]
        for ref in refs[:-3]:
            total = total + ref[...].astype(F32)
        pair_ref[0] = (total * slope_ref[:, :, first : first + width].reshape(rows, width)).astype(BF)
        pair_ref[1] = (total * silu_ref[:, :, first : first + width].reshape(rows, width)).astype(BF)

    args = (mine, *arrived, slope, silu)
    return call(
        kernel, args, [VMEM] * len(args), [VMEM], [struct((2, rows, width))], (6 * mine.size, 16 * mine.size), 6, after
    )


def in_order(core, pairs, after=()):
    half = pairs[0][0].shape[1]
    widths = [mine.shape[2] for mine, _ in pairs]
    n = 2 * len(pairs)

    def kernel(core_ref, *refs):
        ins, outs = refs[:n], refs[n:]

        def put(low):
            at = 0
            for k, width in enumerate(widths):
                for which, ref in enumerate(outs):
                    ref[:half, at : at + width] = ins[2 * k + low][which]
                    ref[half:, at : at + width] = ins[2 * k + 1 - low][which]
                at += width

        @pl.when(core_ref[0] == 0)
        def _():
            put(0)

        @pl.when(core_ref[0] != 0)
        def _():
            put(1)

    shape = struct((2 * half, sum(widths)))
    return call(
        kernel, (core, *[x for pair in pairs for x in pair]), [SMEM] + [VMEM] * n, [VMEM] * 2,
        [shape] * 2, (shape.size, 8 * shape.size), 8, after,
    )


def turned(blocks, codes, after=()):
    rows, width = blocks.arrays[0].shape[1:]
    total = rows * len(codes)

    def kernel(*refs):
        ins, out_ref = refs[:-1], refs[-1]
        for at, size in pieces(width, 512):
            out_ref[at : at + size] = blocks.read(ins, codes, slice(at, at + size)).T

    return call(
        kernel, blocks.arrays, [VMEM] * len(blocks.arrays), [VMEM], [struct((width, total))],
        (total * width, 4 * total * width), 6, after,
    )


def input_part(gate, up, weights, first, wide, rows, groups, place, vmem, after=()):
    tokens, units = gate.shape
    shape = (len(groups[0]), len(groups[0][0]), rows, wide)
    cuts = pieces(wide, 512)
    load = first is not None

    def kernel(gate_ref, up_ref, *refs):
        weight_refs, outs = refs[:2], refs[2:4]
        copies = []
        if load:
            held, sem = refs[4:]
            for i, (at, size) in enumerate(cuts):
                for k in (0, 1):
                    copies.append(
                        pltpu.make_async_copy(
                            weight_refs[k].at[pl.ds(first + at, size)], held.at[k, pl.ds(at, size)], sem.at[k, i]
                        )
                    )
            weight_refs = [held.at[0], held.at[1]]
        for copy in copies[:2]:
            copy.start()
        for i, (at, size) in enumerate(cuts):
            total = 0.0
            for k, ref in enumerate((gate_ref, up_ref)):
                if load:
                    copies[2 * i + k].wait()
                    if 2 * i + k + 2 < len(copies):
                        copies[2 * i + k + 2].start()
                total = total + dot(ref[...], weight_refs[k][at : at + size], NT)
            for ref, group in zip(outs, groups):
                for g, codes in enumerate(group):
                    for j, code in enumerate(codes):
                        b = place[code] * rows
                        ref[g, j, :, at : at + size] = total[b : b + rows].astype(BF)

    return call(
        kernel, (gate, up, *weights), [VMEM] * 2 + [HBM if load else VMEM] * 2, [VMEM] * 2, [struct(shape)] * 2,
        (4 * tokens * units * wide, 4 * units * wide), vmem, after,
        scratch=[pltpu.VMEM((2, wide, units), BF), pltpu.SemaphoreType.DMA((2, len(cuts)))] if load else (), mark=True,
    )


def fold(keep, arrived, after=()):
    def kernel(keep_ref, arrived_ref, a_ref, b_ref):
        a_ref[...] = keep_ref[0] + arrived_ref[0]
        b_ref[...] = keep_ref[1] + arrived_ref[1]

    shape = struct(keep.shape[1:])
    return call(kernel, (keep, arrived), [VMEM] * 2, [VMEM] * 2, [shape, shape], (keep.size, 6 * keep.size), 8, after)


def join(left, left_arrived, right, right_arrived, after=()):
    blocks, rows, wide = left.shape
    half = blocks // 2

    def kernel(a_ref, b_ref, c_ref, d_ref, *outs):
        for k, ref in enumerate(outs):
            at = slice(k * half, (k + 1) * half) if half else slice(None)
            ref[:, :, :wide] = a_ref[at] + b_ref[at]
            ref[:, :, wide:] = c_ref[at] + d_ref[at]

    shape = struct((half or blocks, rows, 2 * wide))
    out = call(
        kernel, (left, left_arrived, right, right_arrived), [VMEM] * 4, [VMEM] * (2 if half else 1),
        [shape] * (2 if half else 1), (left.size * 2, 12 * left.size), 8, after,
    )
    return out if half else (out, None)


def long_product(left, right, begin, end, into=None, after=(), ahead=None, slots=16, vmem=32):
    height, depth = left.shape
    width = right.shape[1]
    cuts = [(begin + at, size) for at, size in pieces(end - begin, 256)]
    slots = min(slots, len(cuts))
    ahead = ahead or []
    n = len(ahead)
    m = 0 if into is None else 1

    def kernel(left_ref, right_ref, *refs):
        sources, (out_ref, *targets), (held, sem, *more) = refs[:n], refs[n + m : 2 * n + m + 1], refs[2 * n + m + 1 :]
        early = [
            pltpu.make_async_copy(a.at[pl.ds(first, count)], b, more[0].at[k])
            for k, (a, b, (_, first, count)) in enumerate(zip(sources, targets, ahead))
        ]
        for copy in early:
            copy.start()
        copies = []
        for i, (at, size) in enumerate(cuts):
            value = dot(left_ref[at : at + size], right_ref[...], NN).astype(BF)
            if i >= slots:
                copies[i - slots].wait()
            held[i % slots, :size] = value
            copies.append(
                pltpu.make_async_copy(held.at[i % slots, pl.ds(0, size)], out_ref.at[pl.ds(at, size)], sem.at[i % slots])
            )
            copies[-1].start()
        for copy in copies[-slots:] + early:
            copy.wait()

    args = [left, right] + [x for x, _, _ in ahead] + ([into] if m else [])
    return call(
        kernel, args, [VMEM] * 2 + [HBM] * (n + m), [HBM] + [VMEM] * n,
        [struct((height, width))] + [struct((count, x.shape[1])) for x, _, count in ahead],
        (2 * depth * width * (end - begin), 2 * width * (end - begin)), vmem, after, {len(args) - 1: 0} if m else None,
        scratch=[pltpu.VMEM((slots, 256, width), BF), pltpu.SemaphoreType.DMA((slots,))]
        + ([pltpu.SemaphoreType.DMA((n,))] if n else []),
        mark=True,
    )


def laid(parts):
    if len(parts) == 1:
        return parts[0]

    def kernel(*refs):
        at = 0
        for ref in refs[:-1]:
            refs[-1][at : at + ref.shape[0]] = ref[...]
            at += ref.shape[0]

    count = sum(x.shape[0] for x in parts)
    return call(
        kernel, parts, [VMEM] * len(parts), [VMEM], [struct((count, *parts[0].shape[1:]))], (0, 4 * count * parts[0].size), 8
    )


def stacked(blocks, codes, after=()):
    rows, width = blocks.arrays[0].shape[1:]
    total = rows * len(codes)

    def kernel(*refs):
        refs[-1][...] = blocks.read(refs[:-1], codes)

    return call(
        kernel, blocks.arrays, [VMEM] * len(blocks.arrays), [VMEM], [struct((total, width))],
        (total * width, 4 * total * width), 8, after,
    )


def on_device(n_row, n_col, tokens, out_grad, gate_saved, up_saved, gate_weight, up_weight, down_weight):
    rows, features = tokens.shape
    units = gate_saved.shape[1]
    row = lax.axis_index("row").astype(jnp.int32)
    core_index = (lax.axis_index("col") % 2).astype(jnp.int32)
    core = core_index.reshape(1)

    def swap(x, mask, axis="row"):
        n = n_row if axis == "row" else n_col
        return lax.ppermute(x, axis, [(i, i ^ mask) for i in range(n)])

    def closure(masks):
        codes = [0]
        for m in masks:
            codes += [c ^ m for c in codes]
        return codes

    def move(codes, mask):
        return [c ^ mask for c in codes]

    masks = [m for m in (1 << i for i in range(1, 31)) if m < n_row]
    low = closure(masks)
    codes = low + move(low, 1)
    place = {c: i for i, c in enumerate(codes)}
    q = len(low)
    order = jnp.array(codes, jnp.int32) ^ row ^ core_index
    places = jnp.arange(2 * q, dtype=jnp.int32) ^ (core_index * q)

    own = out_grad.reshape(1, rows, features)
    held = [(own, [0])]
    for m in masks[:0:-1]:
        held.append((swap(stack([x for x, _ in held]), m), [c ^ m for _, cs in held for c in cs]))
    crossed = swap(own, 1)
    near = [(swap(held[0][0], masks[0]), move(held[0][1], masks[0]))]
    parts = 2 if (units // 2) % 128 == 0 else 1
    width = units // parts
    *weight_rows, mark = brought([(down_weight, k * width, width) for k in range(parts)], 34, (order, places))
    held = held[:1] + [(hold(x, (mark, near[0][0], crossed)), cs) for x, cs in held[1:]]
    near += [(swap(x, masks[0]), move(cs, masks[0])) for x, cs in held[1:]]
    held += near
    grads = Blocks()
    for x, cs in held + [(crossed, [1])] + [(swap(x, 1), move(cs, 1)) for x, cs in held[1:]]:
        grads.add(x, cs)
    hidden_turned, slope, silu = factors(
        order, places, gate_saved.reshape(n_row, rows, units), up_saved.reshape(n_row, rows, units), (near[-1][0],)
    )
    all_grads = stacked(grads, codes, (hidden_turned,))

    all_tokens = Blocks()
    held = [(hold(tokens.reshape(1, rows, features), (near[-1][0],)), [0])]
    for m in masks[::-1]:
        joined = laid([x for x, _ in held])
        held.append((swap(joined, m), [c ^ m for _, cs in held for c in cs]))
    base_crossed = swap(joined, 1)
    crossed = [(base_crossed, [c ^ 1 for _, cs in held[:-1] for c in cs]), (swap(held[-1][0], 1), move(held[-1][1], 1))]
    for x, cs in held + crossed:
        all_tokens.add(x, cs)

    def summed(mine, other, after):
        arrived = [swap(other, 1, "col")]
        sent, m = None, 2
        while m < n_col:
            if len(arrived) > 1:
                mine = mine + arrived.pop(0).astype(F32)
            sent = partial_sum(mine, arrived[-1], after)
            arrived.append(swap(sent, m, "col"))
            m *= 2
        return mine, arrived, sent

    sums, after = [], ()
    for k in range(parts):
        sums.append(hidden_part(core, all_grads, weight_rows[k], after))
        after = (sums[-1][1], all_tokens.arrays[1])
    after = ()
    for k in range(parts):
        sums[k] = summed(*sums[k], after)
        after = (sums[k][2],)

    wide = features // 2
    weights = (gate_weight, up_weight)
    down_grad, a, b, c, d, mark = long_product(
        hidden_turned, all_grads, 0, units, None, (sums[-1][2],),
        [(x, at, wide) for at in (0, wide) for x in weights], 4, 12,
    )
    left_weights, right_weights = (a, b), (c, d)
    pairs = []
    for k, (mine, arrived, _) in enumerate(sums):
        after = (mark, base_crossed, held[-1][0])
        pairs.append(local_grads(mine, arrived, slope, silu, k * width, after))
    gate, up = in_order(core, [(pair, swap(pair, 1, "col")) for pair in pairs])
    tokens_turned = turned(all_tokens, codes)

    rest = closure(masks[1:])
    m = masks[0]
    *left, mark = input_part(
        gate, up, left_weights, None, wide, rows, [[rest, move(rest, m)], [move(rest, 1), move(rest, 1 ^ m)]], place, 7
    )
    *right, mark = input_part(
        gate, up, right_weights, None, wide, rows, [[rest, move(rest, 1)], [move(rest, m), move(rest, m ^ 1)]], place, 7, (mark,)
    )
    some = max(features // 4 // 256 * 256, 256)
    left_got, right_got = swap(left[1], 1), swap(right[1], m)
    gate_grad, mark = long_product(tokens_turned, gate, 0, features - some, None, (mark,))
    left = fold(left[0], left_got, (mark,))
    left_got = swap(left[1], m)
    right = fold(right[0], right_got, (mark, left[1]))
    right_got = swap(right[1], 1)
    gate_grad, mark = long_product(tokens_turned, gate, features - some, features, gate_grad, (left[1], right[1]))
    up_grad, mark = long_product(tokens_turned, up, 0, some, None, (mark,))
    total, sent = join(left[0], left_got, right[0], right_got, (mark,))
    for k, m in enumerate(masks[:0:-1]):
        if k > 0:
            n = total.shape[0] // 2
            total, sent = total[:n], total[n:]
        got = swap(sent, m)
        if k == 0:
            up_grad, _ = long_product(tokens_turned, up, some, features, up_grad, (sent,))
        total = total + got
    return total.reshape(rows, features), gate_grad, up_grad, down_grad


def solution(mesh):
    n_row, n_col = mesh.shape["row"], mesh.shape["col"]
    return jax.shard_map(
        lambda *args: on_device(n_row, n_col, *args),
        mesh=mesh,
        in_specs=(
            P("row", "col"),
            P("row", "col"),
            P(None, "row"),
            P(None, "row"),
            P("col", "row"),
            P("col", "row"),
            P("row", "col"),
        ),
        out_specs=(P("row", "col"), P("col", "row"), P("col", "row"), P("row", "col")),
        check_vma=False,
    )
```

```python
import jax
import jax.numpy as jnp
from jax import lax
from jax.experimental import pallas as pl
from jax.experimental.pallas import tpu as pltpu
from jax.sharding import PartitionSpec as P

BF = jnp.bfloat16
F32 = jnp.float32
NN = (((1,), (0,)), ((), ()))
NT = (((1,), (1,)), ((), ()))
MIB = 1 << 20
VMEM = pl.BlockSpec(memory_space=pltpu.VMEM)
ANY = pl.BlockSpec(memory_space=pl.ANY)
HBM = pl.BlockSpec(memory_space=pltpu.HBM)
SMEM = pl.BlockSpec(memory_space=pltpu.SMEM)


def dot(a, b, dims):
    return lax.dot_general(a, b, dims, preferred_element_type=F32)


def stack(parts):
    return jnp.concatenate(parts, axis=0) if len(parts) > 1 else parts[0]


def pieces(size, step):
    return [(at, min(step, size - at)) for at in range(0, size, step)]


def struct(shape, dtype=BF):
    return jax.ShapeDtypeStruct(tuple(shape), dtype)


def call(kernel, args, in_specs, out_specs, out_shape, cost, vmem, after=(), aliases=None, scratch=(), mark=False):
    n, m = len(args), len(out_shape)

    def body(*refs):
        outs = refs[n + len(after) :]
        if mark:
            outs[m][...] = jnp.zeros((8, 128), F32)
            outs = outs[:m] + outs[m + 1 :]
        kernel(*refs[:n], *outs)

    out = pl.pallas_call(
        body,
        out_shape=list(out_shape) + [struct((8, 128), F32)] * mark,
        in_specs=list(in_specs) + [ANY] * len(after),
        out_specs=list(out_specs) + [VMEM] * mark,
        scratch_shapes=scratch,
        input_output_aliases=aliases or {},
        compiler_params=pltpu.CompilerParams(vmem_limit_bytes=vmem * MIB),
        cost_estimate=pl.CostEstimate(flops=cost[0], bytes_accessed=cost[1], transcendentals=0),
    )(*args, *after)
    return out if len(out) > 1 else out[0]


def hold(x, after):
    def kernel(x_ref, out_ref):
        out_ref[...] = x_ref[...]

    return call(kernel, (x,), [VMEM], [VMEM], [struct(x.shape, x.dtype)], (0, 4 * x.size), 8, after)


def brought(ranges, vmem, after=()):
    n = len(ranges)

    def kernel(*refs):
        copies = [
            pltpu.make_async_copy(refs[k].at[pl.ds(first, count)], refs[n + k], refs[2 * n].at[k])
            for k, (_, first, count) in enumerate(ranges)
        ]
        for copy in copies:
            copy.start()
        for copy in copies:
            copy.wait()

    return call(
        kernel, [x for x, _, _ in ranges], [HBM] * n, [VMEM] * n, [struct((count, x.shape[1])) for x, _, count in ranges],
        (0, sum(2 * count * x.shape[1] for x, _, count in ranges)), vmem, after,
        scratch=[pltpu.SemaphoreType.DMA((n,))], mark=True,
    )


def factors(order, places, gate, up, after=()):
    blocks, rows, width = gate.shape
    half = blocks // 2

    def kernel(order_ref, places_ref, gate_ref, up_ref, turned_ref, slope_ref, silu_ref, held, hidden_ref, sem):
        copies = []
        for i in range(blocks):
            for k, ref in enumerate((gate_ref, up_ref)):
                copies.append(pltpu.make_async_copy(ref.at[order_ref[i]], held.at[k, i], sem.at[k, i]))
                copies[-1].start()
        for i in range(blocks):
            copies[2 * i].wait()
            copies[2 * i + 1].wait()
            g = held[0, i].astype(F32)
            u = held[1, i].astype(F32)
            sig = 1.0 / (1.0 + jnp.exp(-g))
            silu = g * sig
            hidden_ref[places_ref[i]] = (silu * u).astype(BF)
            if i < half:
                silu_ref[i] = silu
                slope_ref[i] = u * sig * (1.0 + g * (1.0 - sig))
        for at, size in pieces(width, 512):
            turned_ref[at : at + size] = stack([hidden_ref[i, :, at : at + size] for i in range(blocks)]).T

    return call(
        kernel, (order, places, gate, up), [SMEM, SMEM, HBM, HBM], [VMEM] * 3,
        [struct((width, blocks * rows)), struct((half, rows, width), F32), struct((half, rows, width), F32)],
        (10 * gate.size, 10 * gate.size), 20, after,
        scratch=[pltpu.VMEM((2, blocks, rows, width), BF), pltpu.VMEM(gate.shape, BF), pltpu.SemaphoreType.DMA((2, blocks))],
    )


class Blocks:
    def __init__(self):
        self.arrays, self.place = [], {}

    def add(self, x, codes):
        for i, code in enumerate(codes):
            self.place[code] = (len(self.arrays), i)
        self.arrays.append(x)

    def read(self, refs, codes, columns=slice(None)):
        return stack([refs[self.place[c][0]][self.place[c][1], :, columns] for c in codes])


def hidden_part(core, grads, weight, after=()):
    half, width = grads.shape[0] // 2, weight.shape[0]

    def kernel(core_ref, grads_ref, weight_ref, mine_ref, other_ref):
        total = dot(grads_ref[...], weight_ref[...], NT)
        is_first = core_ref[0] == 0
        mine_ref[...] = jnp.where(is_first, total[:half], total[half:])
        other_ref[...] = jnp.where(is_first, total[half:], total[:half]).astype(BF)

    return call(
        kernel, (core, grads, weight), [SMEM, VMEM, VMEM], [VMEM] * 2, [struct((half, width), F32), struct((half, width))],
        (4 * half * weight.size, 2 * weight.size), 12, after,
    )


def partial_sum(mine, arrived, after=()):
    def kernel(mine_ref, arrived_ref, out_ref):
        out_ref[...] = (mine_ref[...] + arrived_ref[...].astype(F32)).astype(BF)

    return call(kernel, (mine, arrived), [VMEM] * 2, [VMEM], [struct(mine.shape)], (mine.size, 8 * mine.size), 8, after)


def local_grads(mine, arrived, slope, silu, first, after=()):
    rows, width = mine.shape

    def kernel(mine_ref, *refs):
        slope_ref, silu_ref, pair_ref = refs[-3:]
        total = mine_ref[...]
        for ref in refs[:-3]:
            total = total + ref[...].astype(F32)
        pair_ref[0] = (total * slope_ref[:, :, first : first + width].reshape(rows, width)).astype(BF)
        pair_ref[1] = (total * silu_ref[:, :, first : first + width].reshape(rows, width)).astype(BF)

    args = (mine, *arrived, slope, silu)
    return call(
        kernel, args, [VMEM] * len(args), [VMEM], [struct((2, rows, width))], (6 * mine.size, 16 * mine.size), 6, after
    )


def in_order(core, pairs, after=()):
    half = pairs[0][0].shape[1]
    widths = [mine.shape[2] for mine, _ in pairs]
    n = 2 * len(pairs)

    def kernel(core_ref, *refs):
        ins, outs = refs[:n], refs[n:]

        def put(low):
            at = 0
            for k, width in enumerate(widths):
                for which, ref in enumerate(outs):
                    ref[:half, at : at + width] = ins[2 * k + low][which]
                    ref[half:, at : at + width] = ins[2 * k + 1 - low][which]
                at += width

        @pl.when(core_ref[0] == 0)
        def _():
            put(0)

        @pl.when(core_ref[0] != 0)
        def _():
            put(1)

    shape = struct((2 * half, sum(widths)))
    return call(
        kernel, (core, *[x for pair in pairs for x in pair]), [SMEM] + [VMEM] * n, [VMEM] * 2,
        [shape] * 2, (shape.size, 8 * shape.size), 8, after,
    )


def turned(blocks, codes, after=()):
    rows, width = blocks.arrays[0].shape[1:]
    total = rows * len(codes)

    def kernel(*refs):
        ins, out_ref = refs[:-1], refs[-1]
        for at, size in pieces(width, 512):
            out_ref[at : at + size] = blocks.read(ins, codes, slice(at, at + size)).T

    return call(
        kernel, blocks.arrays, [VMEM] * len(blocks.arrays), [VMEM], [struct((width, total))],
        (total * width, 4 * total * width), 6, after,
    )


def input_part(gate, up, weights, first, wide, rows, groups, place, vmem, after=()):
    tokens, units = gate.shape
    shape = (len(groups[0]), len(groups[0][0]), rows, wide)
    cuts = pieces(wide, 512)
    load = first is not None

    def kernel(gate_ref, up_ref, *refs):
        weight_refs, outs = refs[:2], refs[2:4]
        copies = []
        if load:
            held, sem = refs[4:]
            for i, (at, size) in enumerate(cuts):
                for k in (0, 1):
                    copies.append(
                        pltpu.make_async_copy(
                            weight_refs[k].at[pl.ds(first + at, size)], held.at[k, pl.ds(at, size)], sem.at[k, i]
                        )
                    )
            weight_refs = [held.at[0], held.at[1]]
        for copy in copies[:2]:
            copy.start()
        for i, (at, size) in enumerate(cuts):
            total = 0.0
            for k, ref in enumerate((gate_ref, up_ref)):
                if load:
                    copies[2 * i + k].wait()
                    if 2 * i + k + 2 < len(copies):
                        copies[2 * i + k + 2].start()
                total = total + dot(ref[...], weight_refs[k][at : at + size], NT)
            for ref, group in zip(outs, groups):
                for g, codes in enumerate(group):
                    for j, code in enumerate(codes):
                        b = place[code] * rows
                        ref[g, j, :, at : at + size] = total[b : b + rows].astype(BF)

    return call(
        kernel, (gate, up, *weights), [VMEM] * 2 + [HBM if load else VMEM] * 2, [VMEM] * 2, [struct(shape)] * 2,
        (4 * tokens * units * wide, 4 * units * wide), vmem, after,
        scratch=[pltpu.VMEM((2, wide, units), BF), pltpu.SemaphoreType.DMA((2, len(cuts)))] if load else (), mark=True,
    )


def fold(keep, arrived, after=()):
    def kernel(keep_ref, arrived_ref, a_ref, b_ref):
        a_ref[...] = keep_ref[0] + arrived_ref[0]
        b_ref[...] = keep_ref[1] + arrived_ref[1]

    shape = struct(keep.shape[1:])
    return call(kernel, (keep, arrived), [VMEM] * 2, [VMEM] * 2, [shape, shape], (keep.size, 6 * keep.size), 8, after)


def join(left, left_arrived, right, right_arrived, after=()):
    blocks, rows, wide = left.shape
    half = blocks // 2

    def kernel(a_ref, b_ref, c_ref, d_ref, *outs):
        for k, ref in enumerate(outs):
            at = slice(k * half, (k + 1) * half) if half else slice(None)
            ref[:, :, :wide] = a_ref[at] + b_ref[at]
            ref[:, :, wide:] = c_ref[at] + d_ref[at]

    shape = struct((half or blocks, rows, 2 * wide))
    out = call(
        kernel, (left, left_arrived, right, right_arrived), [VMEM] * 4, [VMEM] * (2 if half else 1),
        [shape] * (2 if half else 1), (left.size * 2, 12 * left.size), 8, after,
    )
    return out if half else (out, None)


def long_product(left, right, begin, end, into=None, after=(), ahead=None, slots=16, vmem=32):
    height, depth = left.shape
    width = right.shape[1]
    cuts = [(begin + at, size) for at, size in pieces(end - begin, 256)]
    slots = min(slots, len(cuts))
    ahead = ahead or []
    n = len(ahead)
    m = 0 if into is None else 1

    def kernel(left_ref, right_ref, *refs):
        sources, (out_ref, *targets), (held, sem, *more) = refs[:n], refs[n + m : 2 * n + m + 1], refs[2 * n + m + 1 :]
        early = [
            pltpu.make_async_copy(a.at[pl.ds(first, count)], b, more[0].at[k])
            for k, (a, b, (_, first, count)) in enumerate(zip(sources, targets, ahead))
        ]
        for copy in early:
            copy.start()
        copies = []
        for i, (at, size) in enumerate(cuts):
            value = dot(left_ref[at : at + size], right_ref[...], NN).astype(BF)
            if i >= slots:
                copies[i - slots].wait()
            held[i % slots, :size] = value
            copies.append(
                pltpu.make_async_copy(held.at[i % slots, pl.ds(0, size)], out_ref.at[pl.ds(at, size)], sem.at[i % slots])
            )
            copies[-1].start()
        for copy in copies[-slots:] + early:
            copy.wait()

    args = [left, right] + [x for x, _, _ in ahead] + ([into] if m else [])
    return call(
        kernel, args, [VMEM] * 2 + [HBM] * (n + m), [HBM] + [VMEM] * n,
        [struct((height, width))] + [struct((count, x.shape[1])) for x, _, count in ahead],
        (2 * depth * width * (end - begin), 2 * width * (end - begin)), vmem, after, {len(args) - 1: 0} if m else None,
        scratch=[pltpu.VMEM((slots, 256, width), BF), pltpu.SemaphoreType.DMA((slots,))]
        + ([pltpu.SemaphoreType.DMA((n,))] if n else []),
        mark=True,
    )


def two_products(left, right, begin, into, next_right, next_end, after=()):
    height, depth = left.shape
    width = right.shape[1]
    cuts = [(0, begin + at, size) for at, size in pieces(height - begin, 256)]
    cuts += [(1, at, size) for at, size in pieces(next_end, 256)]

    def kernel(left_ref, right_ref, next_ref, _, out_ref, next_out_ref, held, sem):
        copies = []
        for i, (k, at, size) in enumerate(cuts):
            held[i, :size] = dot(left_ref[at : at + size], (right_ref, next_ref)[k][...], NN).astype(BF)
            target = (out_ref, next_out_ref)[k]
            copies.append(pltpu.make_async_copy(held.at[i, pl.ds(0, size)], target.at[pl.ds(at, size)], sem.at[i]))
            copies[-1].start()
        for copy in copies:
            copy.wait()

    rows = height - begin + next_end
    return call(
        kernel, (left, right, next_right, into), [VMEM] * 3 + [HBM], [HBM] * 2, [struct((height, width))] * 2,
        (2 * depth * width * rows, 2 * width * rows), 32, after, {3: 0},
        scratch=[pltpu.VMEM((len(cuts), 256, width), BF), pltpu.SemaphoreType.DMA((len(cuts),))], mark=True,
    )


def laid(parts):
    if len(parts) == 1:
        return parts[0]

    def kernel(*refs):
        at = 0
        for ref in refs[:-1]:
            refs[-1][at : at + ref.shape[0]] = ref[...]
            at += ref.shape[0]

    count = sum(x.shape[0] for x in parts)
    return call(
        kernel, parts, [VMEM] * len(parts), [VMEM], [struct((count, *parts[0].shape[1:]))], (0, 4 * count * parts[0].size), 8
    )


def stacked(blocks, codes, after=()):
    rows, width = blocks.arrays[0].shape[1:]
    total = rows * len(codes)

    def kernel(*refs):
        refs[-1][...] = blocks.read(refs[:-1], codes)

    return call(
        kernel, blocks.arrays, [VMEM] * len(blocks.arrays), [VMEM], [struct((total, width))],
        (total * width, 4 * total * width), 8, after,
    )


def on_device(n_row, n_col, tokens, out_grad, gate_saved, up_saved, gate_weight, up_weight, down_weight):
    rows, features = tokens.shape
    units = gate_saved.shape[1]
    row = lax.axis_index("row").astype(jnp.int32)
    core_index = (lax.axis_index("col") % 2).astype(jnp.int32)
    core = core_index.reshape(1)

    def swap(x, mask, axis="row"):
        n = n_row if axis == "row" else n_col
        return lax.ppermute(x, axis, [(i, i ^ mask) for i in range(n)])

    def closure(masks):
        codes = [0]
        for m in masks:
            codes += [c ^ m for c in codes]
        return codes

    def move(codes, mask):
        return [c ^ mask for c in codes]

    masks = [m for m in (1 << i for i in range(1, 31)) if m < n_row]
    low = closure(masks)
    codes = low + move(low, 1)
    place = {c: i for i, c in enumerate(codes)}
    q = len(low)
    order = jnp.array(codes, jnp.int32) ^ row ^ core_index
    places = jnp.arange(2 * q, dtype=jnp.int32) ^ (core_index * q)

    own = out_grad.reshape(1, rows, features)
    held = [(own, [0])]
    for m in masks[:0:-1]:
        held.append((swap(stack([x for x, _ in held]), m), [c ^ m for _, cs in held for c in cs]))
    crossed = swap(own, 1)
    near = [(swap(held[0][0], masks[0]), move(held[0][1], masks[0]))]
    parts = 2 if (units // 2) % 128 == 0 else 1
    width = units // parts
    *weight_rows, mark = brought([(down_weight, k * width, width) for k in range(parts)], 34, (order, places))
    held = held[:1] + [(hold(x, (mark, near[0][0], crossed)), cs) for x, cs in held[1:]]
    near += [(swap(x, masks[0]), move(cs, masks[0])) for x, cs in held[1:]]
    held += near
    grads = Blocks()
    for x, cs in held + [(crossed, [1])] + [(swap(x, 1), move(cs, 1)) for x, cs in held[1:]]:
        grads.add(x, cs)
    hidden_turned, slope, silu = factors(
        order, places, gate_saved.reshape(n_row, rows, units), up_saved.reshape(n_row, rows, units), (near[-1][0],)
    )
    all_grads = stacked(grads, codes, (hidden_turned,))

    all_tokens = Blocks()
    held = [(hold(tokens.reshape(1, rows, features), (near[-1][0],)), [0])]
    for m in masks[::-1]:
        joined = laid([x for x, _ in held])
        held.append((swap(joined, m), [c ^ m for _, cs in held for c in cs]))
    base_crossed = swap(joined, 1)
    crossed = [(base_crossed, [c ^ 1 for _, cs in held[:-1] for c in cs]), (swap(held[-1][0], 1), move(held[-1][1], 1))]
    for x, cs in held + crossed:
        all_tokens.add(x, cs)

    def summed(mine, other, after):
        arrived = [swap(other, 1, "col")]
        sent, m = None, 2
        while m < n_col:
            if len(arrived) > 1:
                mine = mine + arrived.pop(0).astype(F32)
            sent = partial_sum(mine, arrived[-1], after)
            arrived.append(swap(sent, m, "col"))
            m *= 2
        return mine, arrived, sent

    sums, after = [None] * parts, ()
    for k in reversed(range(parts)):
        sums[k] = hidden_part(core, all_grads, weight_rows[k], after)
        after = (sums[k][1], all_tokens.arrays[1])
    after = ()
    for k in reversed(range(parts)):
        sums[k] = summed(*sums[k], after)
        after = (sums[k][2],)

    wide = features // 2
    weights = (gate_weight, up_weight)
    down_grad, a, b, c, d, mark = long_product(
        hidden_turned, all_grads, 0, units, None, (sums[0][2],),
        [(x, at, wide) for at in (0, wide) for x in weights], 4, 12,
    )
    left_weights, right_weights = (a, b), (c, d)
    pairs = []
    for k, (mine, arrived, _) in enumerate(sums):
        after = (mark, base_crossed, held[-1][0])
        pairs.append(local_grads(mine, arrived, slope, silu, k * width, after))
    gate, up = in_order(core, [(pair, swap(pair, 1, "col")) for pair in pairs])
    tokens_turned = turned(all_tokens, codes)

    rest = closure(masks[1:])
    m = masks[0]
    *left, mark = input_part(
        gate, up, left_weights, None, wide, rows, [[rest, move(rest, m)], [move(rest, 1), move(rest, 1 ^ m)]], place, 7
    )
    *right, mark = input_part(
        gate, up, right_weights, None, wide, rows, [[rest, move(rest, 1)], [move(rest, m), move(rest, m ^ 1)]], place, 7, (mark,)
    )
    some = max(features // 4 // 256 * 256, 256)
    left_got, right_got = swap(left[1], 1), swap(right[1], m)
    gate_grad, mark = long_product(tokens_turned, gate, 0, features - some, None, (mark,))
    left = fold(left[0], left_got, (mark,))
    left_got = swap(left[1], m)
    right = fold(right[0], right_got, (mark, left[1]))
    right_got = swap(right[1], 1)
    gate_grad, up_grad, mark = two_products(
        tokens_turned, gate, features - some, gate_grad, up, some, (left[1], right[1])
    )
    total, sent = join(left[0], left_got, right[0], right_got, (mark,))
    for k, m in enumerate(masks[:0:-1]):
        if k > 0:
            n = total.shape[0] // 2
            total, sent = total[:n], total[n:]
        got = swap(sent, m)
        if k == 0:
            up_grad, _ = long_product(tokens_turned, up, some, features, up_grad, (sent,))
        total = total + got
    return total.reshape(rows, features), gate_grad, up_grad, down_grad


def solution(mesh):
    n_row, n_col = mesh.shape["row"], mesh.shape["col"]
    return jax.shard_map(
        lambda *args: on_device(n_row, n_col, *args),
        mesh=mesh,
        in_specs=(
            P("row", "col"),
            P("row", "col"),
            P(None, "row"),
            P(None, "row"),
            P("col", "row"),
            P("col", "row"),
            P("row", "col"),
        ),
        out_specs=(P("row", "col"), P("col", "row"), P("col", "row"), P("row", "col")),
        check_vma=False,
    )
```
